512 devices in a mesh: tm: 32 (over y_lo, z), tensor: 16 (over x, y_hi, core).
Axes of the slice: x: 4, y: 4 (y_hi: 2, y_lo: 2; y = y_hi * 2 + y_lo), z: 16, core: 2. Of those that a mesh axis runs over, the one named last changes fastest.
Arguments:
- patches: bfloat16 [8192, 6144], P('tm', 'tensor'), may hold values from -400 to 400
- ln_gain: float32 [6144], replicated, may hold values from 0.25 to 1.75
- w_query: bfloat16 [6144, 4096], P('tm', 'tensor'), may hold values from -0.05103104 to 0.05103104
- w_key: bfloat16 [6144, 4096], P('tm', 'tensor'), may hold values from -0.053582588 to 0.053582588
- w_value: bfloat16 [6144, 4096], P('tm', 'tensor'), may hold values from -0.078125 to 0.078125
- query_gain: float32 [4096], P('tensor'), may hold values from 0.5 to 21
- key_gain: float32 [4096], P('tensor'), may hold values from 0.5 to 1.5
- w_out: bfloat16 [4096, 6144], P('tensor', 'tm'), may hold values from -0.375 to 0.375
Outputs:
- block_out: bfloat16 [8192, 6144], P('tm', 'tensor')
The draws below stay inside these ranges and needn't reach their ends.
All inputs are finite; a program needn't handle non-finite values.
Results may differ from the reference program's by a relative error of at most 0.019.
Values may be sent and summed in bfloat16 or wider, within the bound.
No kernel may reach another device: no remote copies, remote signals or barrier semaphores. Data moves between devices by JAX's collectives and lax.ppermute only.
A program may use at most 64 MiB of HBM per device.

```python
import jax
import jax.numpy as jnp
from jax import lax

D = 6144
HD = 128
HEADS_DEV = 2
PATCH = 256
FRAMES = 32
TOKENS = 8192
HEADS = 32
HW = 4096
N_TENSOR = 16


def draw_patches(key, part):
    key = jax.random.fold_in(key, 3)
    keys = jax.random.split(key, 3)
    row_scale = jnp.exp(jax.random.uniform(keys[0], (TOKENS, 1)) * jnp.log(10.0))
    col_scale = jnp.exp(jax.random.uniform(keys[1], (1, D)) * jnp.log(10.0))
    base = jnp.clip(jax.random.normal(keys[2], (TOKENS, D)), -4.0, 4.0)
    return (row_scale * col_scale * base).astype(jnp.bfloat16)


def shared_base(key):
    return jnp.clip(jax.random.normal(jax.random.fold_in(key, 7), (D, HW)), -4.0, 4.0) * D ** (-0.5)


def draw_w_query(key, part):
    return shared_base(key).astype(jnp.bfloat16)


def draw_w_key(key, part):
    result = jnp.clip(jax.random.normal(jax.random.fold_in(key, 13), (D, HW)), -4.0, 4.0) * D ** (-0.5)
    return result.astype(jnp.bfloat16)


def draw_query_gain(key, part):
    key = jax.random.fold_in(key, 5)
    keys = jax.random.split(key, 2)
    result = jnp.exp(jax.random.uniform(keys[1], (HW,), minval=-1.0, maxval=1.0) * jnp.log(2.0))
    return result.astype(jnp.float32)


def levels(key, extent, cuts, smallest, high):
    def one(axis_at, shards_of):
        steps = jax.random.uniform(jax.random.fold_in(jax.random.fold_in(key, 6), axis_at), (shards_of,), jnp.float32, smallest / len(cuts), high / len(cuts))
        return jnp.repeat(jnp.exp(steps), extent[axis_at] // shards_of).reshape((-1,) + (1,) * (len(extent) - axis_at - 1))

    loudness = one(*cuts[0])
    for cut in cuts[1:]:
        loudness = loudness * one(*cut)
    return loudness


def noise(key, dims, deviation, limit, cuts=(), kind=jnp.bfloat16):
    entries = deviation * jax.random.normal(key, dims, jnp.float32)
    if cuts:
        entries = entries * levels(key, dims, cuts, -0.22, 0.18)
    return jnp.clip(entries, -limit, limit).astype(kind)


def setup_inputs(seed: int = 0) -> dict:
    splits = jax.random.split(jax.random.key(seed), 9)
    return {
        "patches": draw_patches(jax.random.fold_in(splits[8], 71), 0),
        "ln_gain": jnp.clip(1.0 + 0.15 * jax.random.normal(splits[1], (D,), jnp.float32), 0.25, 1.75),
        "w_query": draw_w_query(jax.random.fold_in(splits[8], 71), 0),
        "w_key": draw_w_key(jax.random.fold_in(splits[8], 71), 0),
        "w_value": noise(splits[4], (D, HW), D ** -0.5, 0.078125, ((0, 32), (1, 16))),
        "query_gain": draw_query_gain(jax.random.fold_in(splits[8], 71), 0),
        "key_gain": jnp.clip(1.0 + 0.1 * jax.random.normal(splits[6], (HW,), jnp.float32), 0.5, 1.5),
        "w_out": noise(splits[7], (HW, D), (HW // 16) ** -0.5, 0.375, ((0, 16), (1, 32))),
    }


epsilon = 1e-06

def layer_norm(values, gain):
    average = lax.optimization_barrier(jnp.mean(values, axis=-1, keepdims=True))
    centred = values - average
    spread = lax.optimization_barrier(jnp.mean(centred * centred, axis=-1, keepdims=True))
    return centred * lax.rsqrt(spread + epsilon) * gain

def head_norm(values, gain):
    shaped = values.reshape(values.shape[0], -1, HD)
    normed = layer_norm(shaped, gain.reshape(-1, HD))
    return normed.reshape(values.shape[0], -1)

def reference(patches, ln_gain, w_query, w_key, w_value, query_gain, key_gain, w_out):
    normed = layer_norm(patches.astype(jnp.float32), ln_gain).astype(jnp.bfloat16)
    q_raw = jnp.dot(normed, w_query, preferred_element_type=jnp.float32)
    query = (head_norm(q_raw, query_gain) * HD ** (-0.5)).astype(jnp.bfloat16)
    k_raw = jnp.dot(normed, w_key, preferred_element_type=jnp.float32)
    key = head_norm(k_raw, key_gain).astype(jnp.bfloat16)
    value = jnp.dot(normed, w_value, preferred_element_type=jnp.float32).astype(jnp.bfloat16)
    query_frames = query.reshape(FRAMES, PATCH, HEADS, HD)
    key_pad = jnp.pad(key.reshape(FRAMES, PATCH, HEADS, HD), ((2, 2), (0, 0), (0, 0), (0, 0)))
    value_pad = jnp.pad(value.reshape(FRAMES, PATCH, HEADS, HD), ((2, 2), (0, 0), (0, 0), (0, 0)))
    offsets = jnp.arange(5 * PATCH, dtype=jnp.int32) // PATCH - 2

    def one_frame(frame_index):
        query_heads = lax.dynamic_index_in_dim(query_frames, frame_index, 0, keepdims=False).astype(jnp.float32)
        key_heads = lax.dynamic_slice_in_dim(key_pad, frame_index, 5, 0).reshape(5 * PATCH, HEADS, HD).astype(jnp.float32)
        value_heads = lax.dynamic_slice_in_dim(value_pad, frame_index, 5, 0).reshape(5 * PATCH, HEADS, HD).astype(jnp.float32)
        seen = frame_index + offsets
        in_clip = (seen >= 0) & (seen < FRAMES)
        scores = jnp.einsum('phd,khd->hpk', query_heads, key_heads)
        scores = jnp.where(in_clip[None, None, :], scores, -jnp.inf)
        top = lax.optimization_barrier(jnp.max(scores, axis=-1, keepdims=True))
        expd = jnp.exp(scores - top)
        row_totals = lax.optimization_barrier(jnp.sum(expd, axis=-1))
        probs = expd.astype(jnp.bfloat16).astype(jnp.float32)
        mixed = jnp.einsum('hpk,khd->phd', probs, value_heads)
        return (mixed / jnp.transpose(row_totals)[:, :, None]).astype(jnp.bfloat16)
    attended = lax.map(one_frame, jnp.arange(FRAMES, dtype=jnp.int32)).reshape(TOKENS, HW)
    group_width = HEADS_DEV * HD
    grouped = jnp.transpose(attended.reshape(TOKENS, N_TENSOR, group_width), (1, 0, 2))
    grouped_w = w_out.reshape(N_TENSOR, group_width, D)

    def add_group(accum, pair):
        partial_value = jnp.dot(pair[0], pair[1], preferred_element_type=jnp.float32).astype(jnp.bfloat16)
        partial_value = lax.optimization_barrier(partial_value)
        return (accum + partial_value.astype(jnp.float32), 0)
    zero_acc = jnp.zeros((TOKENS, D), jnp.float32)
    summed, unused = lax.scan(add_group, zero_acc, (grouped, grouped_w))
    return summed.astype(jnp.bfloat16)
```

```python
import functools

import jax
import jax.numpy as jnp
from jax import lax
from jax.experimental import pallas as pl
from jax.experimental.pallas import tpu as pltpu
from jax.sharding import Mesh
from jax.sharding import PartitionSpec as P

HD = 128
EPS = 1e-06
AXES = ("ylo", "z", "x", "yh", "core")
SIZES = (2, 16, 4, 2, 2)
ROWS = 192
WIDTH = 6144
WINDOW = 9 * 384
BF = jnp.bfloat16
F32 = jnp.float32


def _places():
    for ylo in range(2):
        for z in range(16):
            for x in range(4):
                for yh in range(2):
                    for core in range(2):
                        yield ylo, z, x, yh, core


def _number(ylo, z, x, yh, core):
    return (((ylo * 16 + z) * 4 + x) * 2 + yh) * 2 + core


def send(value, target):
    pairs = [(_number(*p), _number(*target(*p))) for p in _places() if target(*p) is not None]
    return lax.ppermute(value, AXES, pairs)


def along_z(by):
    return lambda ylo, z, x, yh, core: (ylo, (z + by) % 16, x, yh, core)


def other_core(ylo, z, x, yh, core):
    return ylo, z, x, yh, 1 - core


def cross(ylo, z, x, yh, core):
    return (ylo, z, x, yh, 1 - core) if core == ylo else (core, z, x, yh, core)


def from_home(ylo, z, x, yh, core):
    return (ylo, z, x, yh, 1 - core) if core == ylo else None


def onward(ylo, z, x, yh, core):
    return ylo, (z + 1 - 2 * core) % 16, x, yh, core


def out_weight(ylo, z, x, yh, core):
    return core, x * 4 + ((z // 4) % 2) * 2 + z % 2, ylo * 2 + z // 8, yh, (z // 2) % 2


def norm_kernel(place_ref, acts_ref, gain_ref, out_ref):
    ylo, z, core = place_ref[0], place_ref[1], place_ref[4]
    total = jnp.zeros((acts_ref.shape[2], 1), F32)
    for t in range(16):
        total += jnp.sum(acts_ref[0, t].astype(F32), axis=-1, keepdims=True)
    mean = total / WIDTH
    spread = jnp.zeros_like(total)
    for t in range(16):
        centred = acts_ref[0, t].astype(F32) - mean
        spread += jnp.sum(centred * centred, axis=-1, keepdims=True)
    scale = lax.rsqrt(spread / WIDTH + EPS)
    large = lax.rem(z + 8 * (1 - core), 16) // 2
    small = lax.rem(z + 1 + 8 * (1 - core), 16) // 2
    for i in range(9):
        if i < 5:
            t = (ylo ^ core) * 8 + lax.rem(large + i, 8)
        else:
            t = (ylo ^ (1 - core)) * 8 + lax.rem(small + i - 5, 8)
        centred = acts_ref[0, t].astype(F32) - mean
        gain = gain_ref[pl.ds(t, 1), :]
        out_ref[:, i * 384 : (i + 1) * 384] = (centred * scale * gain).astype(BF)


def normalise(place, acts, gain):
    rows = 64
    return pl.pallas_call(
        norm_kernel,
        grid=(2, 256 // rows),
        out_shape=jax.ShapeDtypeStruct((512, WINDOW), BF),
        in_specs=[
            pl.BlockSpec(memory_space=pltpu.SMEM),
            pl.BlockSpec((1, 16, rows, 384), lambda s, r: (s, 0, r, 0)),
            pl.BlockSpec((16, 384), lambda s, r: (0, 0)),
        ],
        out_specs=pl.BlockSpec((rows, WINDOW), lambda s, r: (s * (256 // rows) + r, 0)),
        compiler_params=pltpu.CompilerParams(vmem_limit_bytes=32 << 20),
        cost_estimate=pl.CostEstimate(flops=30_000_000, bytes_accessed=10_000_000, transcendentals=0),
    )(place, acts.reshape(2, 16, 256, 384), gain.reshape(16, 384))


def head_norm(raw, gain):
    mean = jnp.mean(raw, axis=-1, keepdims=True)
    centred = raw - mean
    spread = jnp.mean(centred * centred, axis=-1, keepdims=True)
    return centred * lax.rsqrt(spread + EPS) * gain


def product_kernel(place_ref, normed_ref, *refs):
    first, second, own, last = refs[:7], refs[7:14], refs[14], refs[15]
    mine_ref, theirs_ref, weights, sem = refs[16:]
    core = place_ref[4]

    @pl.when(pl.program_id(0) == 0)
    def _():
        odd = lax.rem(place_ref[1], 2)
        up = core == 0
        blocks = [(own, odd + jnp.where(up, 8, 0)), (last, odd + jnp.where(up, 0, 8))]
        for i in range(7):
            n = i + 1
            blocks.append((first[i], jnp.where(up, odd + 8 - n, 11 - odd + n - 1)))
            blocks.append((second[i], jnp.where(up, 11 - odd + 7 - n, odd + n)))
        copies = []
        for ref, block in blocks:
            rows = pl.ds(pl.multiple_of(block * ROWS, ROWS), ROWS)
            for m in range(3):
                copies.append(pltpu.make_async_copy(ref.at[m], weights.at[rows, pl.ds(m * 256, 256)], sem.at[len(copies)]))
        for copy in copies:
            copy.start()
        for block in (9 * (1 - odd), 10 + 7 * odd):
            weights[pl.ds(pl.multiple_of(block * ROWS, ROWS), ROWS), :] = jnp.zeros((ROWS, 768), BF)
        for copy in copies:
            copy.wait()

    raw = jnp.dot(normed_ref[...], weights[...], preferred_element_type=F32)
    for m in range(3):
        one, two = raw[:, m * 256 : m * 256 + HD], raw[:, m * 256 + HD : (m + 1) * 256]
        mine_ref[:, m * HD : (m + 1) * HD] = jnp.where(core == 0, one, two)
        theirs_ref[:, m * HD : (m + 1) * HD] = jnp.where(core == 0, two, one)


def multiply(place, normed, shards):
    rows = 128
    return pl.pallas_call(
        product_kernel,
        grid=(512 // rows,),
        out_shape=[jax.ShapeDtypeStruct((512, 3 * HD), F32)] * 2,
        in_specs=[pl.BlockSpec(memory_space=pltpu.SMEM), pl.BlockSpec((rows, WINDOW), lambda r: (r, 0))]
        + [pl.BlockSpec(memory_space=pl.ANY)] * 16,
        out_specs=[pl.BlockSpec((rows, 3 * HD), lambda r: (r, 0))] * 2,
        scratch_shapes=[pltpu.VMEM((WINDOW, 768), BF), pltpu.SemaphoreType.DMA((48,))],
        compiler_params=pltpu.CompilerParams(vmem_limit_bytes=32 << 20),
        cost_estimate=pl.CostEstimate(flops=2 * 512 * WINDOW * 768, bytes_accessed=10_000_000, transcendentals=0),
    )(place, normed, *shards)


def heads_kernel(mine_ref, theirs_ref, gains_ref, q_ref, kv_ref):
    raw = mine_ref[...] + theirs_ref[...]
    query = head_norm(raw[:, :HD], gains_ref[0:1, :]) * HD ** (-0.5)
    q_ref[...] = query.astype(BF)
    kv_ref[0] = head_norm(raw[:, HD : 2 * HD], gains_ref[1:2, :]).astype(BF)
    kv_ref[1] = raw[:, 2 * HD :].astype(BF)


def split_heads(mine, theirs, gains):
    return pl.pallas_call(
        heads_kernel,
        out_shape=(jax.ShapeDtypeStruct((512, HD), BF), jax.ShapeDtypeStruct((2, 512, HD), BF)),
        in_specs=[pl.BlockSpec(memory_space=pltpu.VMEM)] * 3,
        out_specs=(pl.BlockSpec(memory_space=pltpu.VMEM), pl.BlockSpec(memory_space=pltpu.VMEM)),
        compiler_params=pltpu.CompilerParams(vmem_limit_bytes=32 << 20),
        cost_estimate=pl.CostEstimate(flops=4_000_000, bytes_accessed=2_000_000, transcendentals=0),
    )(mine, theirs, gains)


def attend_kernel(place_ref, q_ref, *refs):
    kvs, out_ref = refs[:5], refs[5]
    z = place_ref[1]
    for slot in range(2):
        query = q_ref[slot * 256 : (slot + 1) * 256, :]
        scores = []
        starts = []
        for offset, ref in zip((-2, -1, 0, 1, 2), kvs, strict=True):
            wrap = jnp.where(z + offset < 0, -1, jnp.where(z + offset >= 16, 1, 0))
            held = slot + wrap
            valid = (held >= 0) & (held < 2)
            start = pl.multiple_of(jnp.clip(held, 0, 1) * 256, 256)
            starts.append(start)
            key = ref[0, pl.ds(start, 256), :]
            part = lax.dot_general(query, key, (((1,), (1,)), ((), ())), preferred_element_type=F32)
            scores.append(part + jnp.where(valid, 0.0, -jnp.inf))
        top = scores[0]
        for part in scores[1:]:
            top = jnp.maximum(top, part)
        top = jnp.max(top, axis=-1, keepdims=True)
        total = jnp.zeros((256, 1), F32)
        mixed = jnp.zeros((256, HD), F32)
        for part, start, ref in zip(scores, starts, kvs, strict=True):
            expd = jnp.exp(part - top)
            total += jnp.sum(expd, axis=-1, keepdims=True)
            value = ref[1, pl.ds(start, 256), :]
            mixed += jnp.dot(expd.astype(BF), value, preferred_element_type=F32)
        result = (mixed / total).astype(BF)
        for copy in range(8):
            out_ref[copy, slot * 256 : (slot + 1) * 256, :] = result


def attend(place, query, kvs):
    return pl.pallas_call(
        attend_kernel,
        out_shape=jax.ShapeDtypeStruct((8, 512, HD), BF),
        in_specs=[pl.BlockSpec(memory_space=pltpu.SMEM)] + [pl.BlockSpec(memory_space=pltpu.VMEM)] * 6,
        out_specs=pl.BlockSpec(memory_space=pltpu.VMEM),
        compiler_params=pltpu.CompilerParams(vmem_limit_bytes=32 << 20),
        cost_estimate=pl.CostEstimate(flops=4 * 512 * 1280 * HD, bytes_accessed=1_600_000, transcendentals=512 * 1280),
    )(place, query, *kvs)


def out_kernel(heads_ref, weights_ref, out_ref):
    for slot in range(2):
        part = jnp.zeros((256, 768), F32)
        for x in range(4):
            rows = slice(slot * 256, (slot + 1) * 256)
            pair = jnp.concatenate([heads_ref[2 * x, rows, :], heads_ref[2 * x + 1, rows, :]], axis=1)
            part += lax.dot_general(pair, weights_ref[x], (((1,), (1,)), ((), ())), preferred_element_type=F32)
        out_ref[slot] = part[:, :384].astype(BF)
        out_ref[2 + slot] = part[:, 384:].astype(BF)


def project_out(heads, weights):
    return pl.pallas_call(
        out_kernel,
        out_shape=jax.ShapeDtypeStruct((4, 256, 384), BF),
        in_specs=[pl.BlockSpec(memory_space=pltpu.VMEM)] * 2,
        out_specs=pl.BlockSpec(memory_space=pltpu.VMEM),
        compiler_params=pltpu.CompilerParams(vmem_limit_bytes=32 << 20),
        cost_estimate=pl.CostEstimate(flops=2 * 512 * 768 * 1024, bytes_accessed=3_500_000, transcendentals=0),
    )(heads, weights)


def per_device(patches, ln_gain, w_query, w_key, w_value, query_gain, key_gain, w_out):
    place = jnp.stack([lax.axis_index(a) for a in AXES]).astype(jnp.int32)
    ylo, core = place[0], place[4]
    home = core == ylo
    acts = lax.all_gather(patches, ("ylo", "x", "yh", "core"), axis=0, tiled=False)

    held = jnp.stack([w_query, w_key, w_value])
    got = send(held, cross)
    one = jnp.where(home, held, got)
    two = jnp.where(home, got, send(got, from_home))
    shards = [[], []]
    ends = [one, two]
    for step in range(7):
        for chain in range(2):
            ends[chain] = send(ends[chain], onward)
            shards[chain].append(ends[chain])
    last = send(jnp.where(core == 0, ends[0], ends[1]), onward)
    own = jnp.where(core == 0, one, two)

    turned = send(w_out.T, out_weight)
    out_weights = lax.all_gather(turned, "z", axis=0, tiled=False).reshape(4, 768, 256)

    normed = normalise(place, acts, ln_gain)
    mine, theirs = multiply(place, normed, shards[0] + shards[1] + [own, last])
    gains = jnp.stack([query_gain, key_gain])
    gains = jnp.where(home, gains, send(gains, other_core)).reshape(2, 2, HD)
    gains = jnp.where(core == 0, gains[:, 0], gains[:, 1])
    query, kv = split_heads(mine, send(theirs, other_core), gains)
    near = {offset: send(kv, along_z(-offset)) for offset in (-2, 2, -1, 1)}
    near[0] = kv
    attended = attend(place, query, [near[o] for o in (-2, -1, 0, 1, 2)])
    heads = lax.all_to_all(attended, ("x", "core"), 0, 0, tiled=True)
    parts = project_out(heads, out_weights)
    parts = lax.all_to_all(parts, ("yh", "ylo"), 0, 0, tiled=True)
    return jnp.sum(parts.astype(F32), axis=0).astype(BF)


def solution(mesh):
    fine = Mesh(mesh.devices.reshape(SIZES), AXES)
    tm, tensor = ("ylo", "z"), ("x", "yh", "core")
    return jax.shard_map(
        per_device,
        mesh=fine,
        in_specs=(
            P(tm, tensor),
            P(),
            P(tm, tensor),
            P(tm, tensor),
            P(tm, tensor),
            P(tensor),
            P(tensor),
            P(tensor, tm),
        ),
        out_specs=P(tm, tensor),
        check_vma=False,
    )
```

```python
import functools

import jax
import jax.numpy as jnp
from jax import lax
from jax.experimental import pallas as pl
from jax.experimental.pallas import tpu as pltpu
from jax.sharding import Mesh
from jax.sharding import PartitionSpec as P

HD = 128
EPS = 1e-06
AXES = ("ylo", "z", "x", "yh", "core")
SIZES = (2, 16, 4, 2, 2)
ROWS = 192
WIDTH = 6144
WINDOW = 9 * 384
BF = jnp.bfloat16
F32 = jnp.float32


def _places():
    for ylo in range(2):
        for z in range(16):
            for x in range(4):
                for yh in range(2):
                    for core in range(2):
                        yield ylo, z, x, yh, core


def _number(ylo, z, x, yh, core):
    return (((ylo * 16 + z) * 4 + x) * 2 + yh) * 2 + core


def send(value, target):
    pairs = [(_number(*p), _number(*target(*p))) for p in _places() if target(*p) is not None]
    return lax.ppermute(value, AXES, pairs)


def along_z(by):
    return lambda ylo, z, x, yh, core: (ylo, (z + by) % 16, x, yh, core)


def other_core(ylo, z, x, yh, core):
    return ylo, z, x, yh, 1 - core


def cross(ylo, z, x, yh, core):
    return (ylo, z, x, yh, 1 - core) if core == ylo else (core, z, x, yh, core)


def from_home(ylo, z, x, yh, core):
    return (ylo, z, x, yh, 1 - core) if core == ylo else None


def onward(ylo, z, x, yh, core):
    return ylo, (z + 1 - 2 * core) % 16, x, yh, core


def out_weight(ylo, z, x, yh, core):
    low = z % 8
    nearby = z - low - 4 + 4 * (low % 2 + 2 * (low // 4)) + x
    return core, nearby % 16, ylo * 2 + z // 8, yh, (z // 2) % 2


def norm_kernel(place_ref, acts_ref, gain_ref, out_ref):
    ylo, z, core = place_ref[0], place_ref[1], place_ref[4]
    total = jnp.zeros((acts_ref.shape[2], 1), F32)
    for t in range(16):
        total += jnp.sum(acts_ref[0, t].astype(F32), axis=-1, keepdims=True)
    mean = total / WIDTH
    spread = jnp.zeros_like(total)
    for t in range(16):
        centred = acts_ref[0, t].astype(F32) - mean
        spread += jnp.sum(centred * centred, axis=-1, keepdims=True)
    scale = lax.rsqrt(spread / WIDTH + EPS)
    large = lax.rem(z + 8 * (1 - core), 16) // 2
    small = lax.rem(z + 1 + 8 * (1 - core), 16) // 2
    for i in range(9):
        if i < 5:
            t = (ylo ^ core) * 8 + lax.rem(large + i, 8)
        else:
            t = (ylo ^ (1 - core)) * 8 + lax.rem(small + i - 5, 8)
        centred = acts_ref[0, t].astype(F32) - mean
        gain = gain_ref[pl.ds(t, 1), :]
        out_ref[:, i * 384 : (i + 1) * 384] = (centred * scale * gain).astype(BF)


def normalise(place, acts, gain):
    rows = 64
    return pl.pallas_call(
        norm_kernel,
        grid=(2, 256 // rows),
        out_shape=jax.ShapeDtypeStruct((512, WINDOW), BF),
        in_specs=[
            pl.BlockSpec(memory_space=pltpu.SMEM),
            pl.BlockSpec((1, 16, rows, 384), lambda s, r: (s, 0, r, 0)),
            pl.BlockSpec((16, 384), lambda s, r: (0, 0)),
        ],
        out_specs=pl.BlockSpec((rows, WINDOW), lambda s, r: (s * (256 // rows) + r, 0)),
        compiler_params=pltpu.CompilerParams(vmem_limit_bytes=32 << 20),
        cost_estimate=pl.CostEstimate(flops=30_000_000, bytes_accessed=10_000_000, transcendentals=0),
    )(place, acts.reshape(2, 16, 256, 384), gain.reshape(16, 384))


def head_norm(raw, gain):
    mean = jnp.mean(raw, axis=-1, keepdims=True)
    centred = raw - mean
    spread = jnp.mean(centred * centred, axis=-1, keepdims=True)
    return centred * lax.rsqrt(spread + EPS) * gain


def product_kernel(place_ref, normed_ref, *refs):
    first, second, own, last = refs[:7], refs[7:14], refs[14], refs[15]
    mine_ref, theirs_ref, weights, sem = refs[16:]
    core = place_ref[4]

    @pl.when(pl.program_id(0) == 0)
    def _():
        odd = lax.rem(place_ref[1], 2)
        up = core == 0
        blocks = [(own, odd + jnp.where(up, 8, 0)), (last, odd + jnp.where(up, 0, 8))]
        for i in range(7):
            n = i + 1
            blocks.append((first[i], jnp.where(up, odd + 8 - n, 11 - odd + n - 1)))
            blocks.append((second[i], jnp.where(up, 11 - odd + 7 - n, odd + n)))
        copies = []
        for ref, block in blocks:
            rows = pl.ds(pl.multiple_of(block * ROWS, ROWS), ROWS)
            for m in range(3):
                copies.append(pltpu.make_async_copy(ref.at[m], weights.at[rows, pl.ds(m * 256, 256)], sem.at[len(copies)]))
        for copy in copies:
            copy.start()
        for block in (9 * (1 - odd), 10 + 7 * odd):
            weights[pl.ds(pl.multiple_of(block * ROWS, ROWS), ROWS), :] = jnp.zeros((ROWS, 768), BF)
        for copy in copies:
            copy.wait()

    raw = jnp.dot(normed_ref[...], weights[...], preferred_element_type=F32)
    for m in range(3):
        one, two = raw[:, m * 256 : m * 256 + HD], raw[:, m * 256 + HD : (m + 1) * 256]
        mine_ref[:, m * HD : (m + 1) * HD] = jnp.where(core == 0, one, two)
        theirs_ref[:, m * HD : (m + 1) * HD] = jnp.where(core == 0, two, one)


def multiply(place, normed, shards):
    rows = 128
    return pl.pallas_call(
        product_kernel,
        grid=(512 // rows,),
        out_shape=[jax.ShapeDtypeStruct((512, 3 * HD), F32)] * 2,
        in_specs=[pl.BlockSpec(memory_space=pltpu.SMEM), pl.BlockSpec((rows, WINDOW), lambda r: (r, 0))]
        + [pl.BlockSpec(memory_space=pl.ANY)] * 16,
        out_specs=[pl.BlockSpec((rows, 3 * HD), lambda r: (r, 0))] * 2,
        scratch_shapes=[pltpu.VMEM((WINDOW, 768), BF), pltpu.SemaphoreType.DMA((48,))],
        compiler_params=pltpu.CompilerParams(vmem_limit_bytes=32 << 20),
        cost_estimate=pl.CostEstimate(flops=2 * 512 * WINDOW * 768, bytes_accessed=10_000_000, transcendentals=0),
    )(place, normed, *shards)


def heads_kernel(mine_ref, theirs_ref, gains_ref, q_ref, kv_ref):
    raw = mine_ref[...] + theirs_ref[...]
    query = head_norm(raw[:, :HD], gains_ref[0:1, :]) * HD ** (-0.5)
    q_ref[...] = query.astype(BF)
    kv_ref[0] = head_norm(raw[:, HD : 2 * HD], gains_ref[1:2, :]).astype(BF)
    kv_ref[1] = raw[:, 2 * HD :].astype(BF)


def split_heads(mine, theirs, gains):
    return pl.pallas_call(
        heads_kernel,
        out_shape=(jax.ShapeDtypeStruct((512, HD), BF), jax.ShapeDtypeStruct((2, 512, HD), BF)),
        in_specs=[pl.BlockSpec(memory_space=pltpu.VMEM)] * 3,
        out_specs=(pl.BlockSpec(memory_space=pltpu.VMEM), pl.BlockSpec(memory_space=pltpu.VMEM)),
        compiler_params=pltpu.CompilerParams(vmem_limit_bytes=32 << 20),
        cost_estimate=pl.CostEstimate(flops=4_000_000, bytes_accessed=2_000_000, transcendentals=0),
    )(mine, theirs, gains)


def attend_kernel(place_ref, q_ref, *refs):
    kvs, out_ref = refs[:5], refs[5]
    z = place_ref[1]
    for slot in range(2):
        query = q_ref[slot * 256 : (slot + 1) * 256, :]
        scores = []
        starts = []
        for offset, ref in zip((-2, -1, 0, 1, 2), kvs, strict=True):
            wrap = jnp.where(z + offset < 0, -1, jnp.where(z + offset >= 16, 1, 0))
            held = slot + wrap
            valid = (held >= 0) & (held < 2)
            start = pl.multiple_of(jnp.clip(held, 0, 1) * 256, 256)
            starts.append(start)
            key = ref[0, pl.ds(start, 256), :]
            part = lax.dot_general(query, key, (((1,), (1,)), ((), ())), preferred_element_type=F32)
            scores.append(part + jnp.where(valid, 0.0, -jnp.inf))
        top = scores[0]
        for part in scores[1:]:
            top = jnp.maximum(top, part)
        top = jnp.max(top, axis=-1, keepdims=True)
        total = jnp.zeros((256, 1), F32)
        mixed = jnp.zeros((256, HD), F32)
        for part, start, ref in zip(scores, starts, kvs, strict=True):
            expd = jnp.exp(part - top)
            total += jnp.sum(expd, axis=-1, keepdims=True)
            value = ref[1, pl.ds(start, 256), :]
            mixed += jnp.dot(expd.astype(BF), value, preferred_element_type=F32)
        result = (mixed / total).astype(BF)
        for copy in range(8):
            out_ref[copy, slot * 256 : (slot + 1) * 256, :] = result


def attend(place, query, kvs):
    return pl.pallas_call(
        attend_kernel,
        out_shape=jax.ShapeDtypeStruct((8, 512, HD), BF),
        in_specs=[pl.BlockSpec(memory_space=pltpu.SMEM)] + [pl.BlockSpec(memory_space=pltpu.VMEM)] * 6,
        out_specs=pl.BlockSpec(memory_space=pltpu.VMEM),
        compiler_params=pltpu.CompilerParams(vmem_limit_bytes=32 << 20),
        cost_estimate=pl.CostEstimate(flops=4 * 512 * 1280 * HD, bytes_accessed=1_600_000, transcendentals=512 * 1280),
    )(place, query, *kvs)


def out_kernel(place_ref, heads_ref, weights_ref, out_ref):
    corner = 12 + 8 * lax.rem(place_ref[2], 2)
    for slot in range(2):
        part = jnp.zeros((256, 768), F32)
        for x in range(4):
            rows = slice(slot * 256, (slot + 1) * 256)
            pair = jnp.concatenate([heads_ref[2 * x, rows, :], heads_ref[2 * x + 1, rows, :]], axis=1)
            block = jnp.concatenate([weights_ref[lax.rem(corner + 4 * r + x, 16)] for r in range(4)], axis=0)
            part += lax.dot_general(pair, block, (((1,), (1,)), ((), ())), preferred_element_type=F32)
        out_ref[slot] = part[:, :384].astype(BF)
        out_ref[2 + slot] = part[:, 384:].astype(BF)


def project_out(place, heads, weights):
    return pl.pallas_call(
        out_kernel,
        out_shape=jax.ShapeDtypeStruct((4, 256, 384), BF),
        in_specs=[pl.BlockSpec(memory_space=pltpu.SMEM)] + [pl.BlockSpec(memory_space=pltpu.VMEM)] * 2,
        out_specs=pl.BlockSpec(memory_space=pltpu.VMEM),
        compiler_params=pltpu.CompilerParams(vmem_limit_bytes=32 << 20),
        cost_estimate=pl.CostEstimate(flops=2 * 512 * 768 * 1024, bytes_accessed=3_500_000, transcendentals=0),
    )(place, heads, weights)


def per_device(patches, ln_gain, w_query, w_key, w_value, query_gain, key_gain, w_out):
    place = jnp.stack([lax.axis_index(a) for a in AXES]).astype(jnp.int32)
    ylo, core = place[0], place[4]
    home = core == ylo
    acts = lax.all_gather(patches, ("ylo", "x", "yh", "core"), axis=0, tiled=False)

    held = jnp.stack([w_query, w_key, w_value])
    got = send(held, cross)
    one = jnp.where(home, held, got)
    two = jnp.where(home, got, send(got, from_home))
    shards = [[], []]
    ends = [one, two]
    for step in range(7):
        for chain in range(2):
            ends[chain] = send(ends[chain], onward)
            shards[chain].append(ends[chain])
    last = send(jnp.where(core == 0, ends[0], ends[1]), onward)
    own = jnp.where(core == 0, one, two)

    turned = send(w_out.T, out_weight)
    out_weights = lax.all_gather(turned, "z", axis=0, tiled=False)

    normed = normalise(place, acts, ln_gain)
    mine, theirs = multiply(place, normed, shards[0] + shards[1] + [own, last])
    gains = jnp.stack([query_gain, key_gain])
    gains = jnp.where(home, gains, send(gains, other_core)).reshape(2, 2, HD)
    gains = jnp.where(core == 0, gains[:, 0], gains[:, 1])
    query, kv = split_heads(mine, send(theirs, other_core), gains)
    near = {offset: send(kv, along_z(-offset)) for offset in (-2, 2, -1, 1)}
    near[0] = kv
    attended = attend(place, query, [near[o] for o in (-2, -1, 0, 1, 2)])
    heads = lax.all_to_all(attended, ("x", "core"), 0, 0, tiled=True)
    parts = project_out(place, heads, out_weights)
    parts = lax.all_to_all(parts, ("yh", "ylo"), 0, 0, tiled=True)
    return jnp.sum(parts.astype(F32), axis=0).astype(BF)


def solution(mesh):
    fine = Mesh(mesh.devices.reshape(SIZES), AXES)
    tm, tensor = ("ylo", "z"), ("x", "yh", "core")
    return jax.shard_map(
        per_device,
        mesh=fine,
        in_specs=(
            P(tm, tensor),
            P(),
            P(tm, tensor),
            P(tm, tensor),
            P(tm, tensor),
            P(tensor),
            P(tensor),
            P(tensor, tm),
        ),
        out_specs=P(tm, tensor),
        check_vma=False,
    )
```

```python
import functools

import jax
import jax.numpy as jnp
from jax import lax
from jax.experimental import pallas as pl
from jax.experimental.pallas import tpu as pltpu
from jax.sharding import Mesh
from jax.sharding import PartitionSpec as P

HD = 128
EPS = 1e-06
AXES = ("ylo", "z", "x", "yh", "core")
SIZES = (2, 16, 4, 2, 2)
ROWS = 192
WIDTH = 6144
WINDOW = 9 * 384
BF = jnp.bfloat16
F32 = jnp.float32


def _places():
    for ylo in range(2):
        for z in range(16):
            for x in range(4):
                for yh in range(2):
                    for core in range(2):
                        yield ylo, z, x, yh, core


def _number(ylo, z, x, yh, core):
    return (((ylo * 16 + z) * 4 + x) * 2 + yh) * 2 + core


def send(value, target):
    pairs = [(_number(*p), _number(*target(*p))) for p in _places() if target(*p) is not None]
    return lax.ppermute(value, AXES, pairs)


def along_z(by):
    return lambda ylo, z, x, yh, core: (ylo, (z + by) % 16, x, yh, core)


def other_core(ylo, z, x, yh, core):
    return ylo, z, x, yh, 1 - core


def cross(ylo, z, x, yh, core):
    return (ylo, z, x, yh, 1 - core) if core == ylo else (core, z, x, yh, core)


def from_home(ylo, z, x, yh, core):
    return (ylo, z, x, yh, 1 - core) if core == ylo else None


def onward(ylo, z, x, yh, core):
    return ylo, (z + 1 - 2 * core) % 16, x, yh, core


def out_weight(ylo, z, x, yh, core):
    low = z % 8
    nearby = z - low - 4 + 4 * (low % 2 + 2 * (low // 4)) + x
    return core, nearby % 16, ylo * 2 + z // 8, yh, (z // 2) % 2


def norm_kernel(place_ref, acts_ref, gain_ref, out_ref):
    ylo, z, core = place_ref[0], place_ref[1], place_ref[4]
    total = jnp.zeros((acts_ref.shape[2], 1), F32)
    for t in range(16):
        total += jnp.sum(acts_ref[0, t].astype(F32), axis=-1, keepdims=True)
    mean = total / WIDTH
    spread = jnp.zeros_like(total)
    for t in range(16):
        centred = acts_ref[0, t].astype(F32) - mean
        spread += jnp.sum(centred * centred, axis=-1, keepdims=True)
    scale = lax.rsqrt(spread / WIDTH + EPS)
    large = lax.rem(z + 8 * (1 - core), 16) // 2
    small = lax.rem(z + 1 + 8 * (1 - core), 16) // 2
    for i in range(9):
        if i < 5:
            t = (ylo ^ core) * 8 + lax.rem(large + i, 8)
        else:
            t = (ylo ^ (1 - core)) * 8 + lax.rem(small + i - 5, 8)
        centred = acts_ref[0, t].astype(F32) - mean
        gain = gain_ref[pl.ds(t, 1), :]
        out_ref[:, i * 384 : (i + 1) * 384] = (centred * scale * gain).astype(BF)


def normalise(place, acts, gain):
    rows = 64
    return pl.pallas_call(
        norm_kernel,
        grid=(2, 256 // rows),
        out_shape=jax.ShapeDtypeStruct((512, WINDOW), BF),
        in_specs=[
            pl.BlockSpec(memory_space=pltpu.SMEM),
            pl.BlockSpec((1, 16, rows, 384), lambda s, r: (s, 0, r, 0)),
            pl.BlockSpec((16, 384), lambda s, r: (0, 0)),
        ],
        out_specs=pl.BlockSpec((rows, WINDOW), lambda s, r: (s * (256 // rows) + r, 0)),
        compiler_params=pltpu.CompilerParams(vmem_limit_bytes=32 << 20),
        cost_estimate=pl.CostEstimate(flops=30_000_000, bytes_accessed=10_000_000, transcendentals=0),
    )(place, acts.reshape(2, 16, 256, 384), gain.reshape(16, 384))


def head_norm(raw, gain):
    mean = jnp.mean(raw, axis=-1, keepdims=True)
    centred = raw - mean
    spread = jnp.mean(centred * centred, axis=-1, keepdims=True)
    return centred * lax.rsqrt(spread + EPS) * gain


def product_kernel(place_ref, gains_ref, normed_ref, *refs):
    first, second, own, last = refs[:7], refs[7:14], refs[14], refs[15]
    mine_ref, theirs_ref, weights, sem = refs[16:]
    core = place_ref[4]

    @pl.when(pl.program_id(0) == 0)
    def _():
        odd = lax.rem(place_ref[1], 2)
        up = core == 0
        blocks = [(own, odd + jnp.where(up, 8, 0)), (last, odd + jnp.where(up, 0, 8))]
        for i in range(7):
            n = i + 1
            blocks.append((first[i], jnp.where(up, odd + 8 - n, 11 - odd + n - 1)))
            blocks.append((second[i], jnp.where(up, 11 - odd + 7 - n, odd + n)))
        copies = []
        for ref, block in blocks:
            rows = pl.ds(pl.multiple_of(block * ROWS, ROWS), ROWS)
            for m in range(3):
                copies.append(pltpu.make_async_copy(ref.at[m], weights.at[rows, pl.ds(m * 256, 256)], sem.at[len(copies)]))
        for copy in copies:
            copy.start()
        for block in (9 * (1 - odd), 10 + 7 * odd):
            weights[pl.ds(pl.multiple_of(block * ROWS, ROWS), ROWS), :] = jnp.zeros((ROWS, 768), BF)
        for copy in copies:
            copy.wait()

    raw = jnp.dot(normed_ref[...], weights[...], preferred_element_type=F32)
    for m in range(3):
        one, two = raw[:, m * 256 : m * 256 + HD], raw[:, m * 256 + HD : (m + 1) * 256]
        mine_ref[:, m * HD : (m + 1) * HD] = jnp.where(core == 0, one, two)
        theirs_ref[:128, m * HD : (m + 1) * HD] = jnp.where(core == 0, two, one)
    theirs_ref[128:, :] = gains_ref[...]


def multiply(place, gains, normed, shards):
    rows = 128
    return pl.pallas_call(
        product_kernel,
        grid=(512 // rows,),
        out_shape=[jax.ShapeDtypeStruct((512, 3 * HD), F32), jax.ShapeDtypeStruct((544, 3 * HD), F32)],
        in_specs=[pl.BlockSpec(memory_space=pltpu.SMEM), pl.BlockSpec((8, 3 * HD), lambda r: (0, 0)), pl.BlockSpec((rows, WINDOW), lambda r: (r, 0))]
        + [pl.BlockSpec(memory_space=pl.ANY)] * 16,
        out_specs=[pl.BlockSpec((n, 3 * HD), lambda r: (r, 0)) for n in (rows, rows + 8)],
        scratch_shapes=[pltpu.VMEM((WINDOW, 768), BF), pltpu.SemaphoreType.DMA((48,))],
        compiler_params=pltpu.CompilerParams(vmem_limit_bytes=32 << 20),
        cost_estimate=pl.CostEstimate(flops=2 * 512 * WINDOW * 768, bytes_accessed=10_000_000, transcendentals=0),
    )(place, gains, normed, *shards)


def heads_kernel(place_ref, mine_ref, theirs_ref, gains_ref, q_ref, kv_ref):
    ylo, core = place_ref[0], place_ref[4]
    pair = jnp.where(core == ylo, gains_ref[0:2, :256], theirs_ref[0, 128:130, :256])
    gains = jnp.where(core == 0, pair[:, :HD], pair[:, HD:])
    for r in range(4):
        rows = slice(r * 128, (r + 1) * 128)
        raw = mine_ref[rows, :] + theirs_ref[r, :128, :]
        query = head_norm(raw[:, :HD], gains[0:1, :]) * HD ** (-0.5)
        q_ref[rows, :] = query.astype(BF)
        kv_ref[0, rows, :] = head_norm(raw[:, HD : 2 * HD], gains[1:2, :]).astype(BF)
        kv_ref[1, rows, :] = raw[:, 2 * HD :].astype(BF)


def split_heads(place, mine, theirs, gains):
    return pl.pallas_call(
        heads_kernel,
        out_shape=(jax.ShapeDtypeStruct((512, HD), BF), jax.ShapeDtypeStruct((2, 512, HD), BF)),
        in_specs=[pl.BlockSpec(memory_space=pltpu.SMEM)] + [pl.BlockSpec(memory_space=pltpu.VMEM)] * 3,
        out_specs=(pl.BlockSpec(memory_space=pltpu.VMEM), pl.BlockSpec(memory_space=pltpu.VMEM)),
        compiler_params=pltpu.CompilerParams(vmem_limit_bytes=32 << 20),
        cost_estimate=pl.CostEstimate(flops=4_000_000, bytes_accessed=2_000_000, transcendentals=0),
    )(place, mine, theirs.reshape(4, 136, 3 * HD), gains)


def attend_kernel(place_ref, q_ref, *refs):
    kvs, out_ref = refs[:5], refs[5]
    z = place_ref[1]
    for slot in range(2):
        query = q_ref[slot * 256 : (slot + 1) * 256, :]
        scores = []
        starts = []
        for offset, ref in zip((-2, -1, 0, 1, 2), kvs, strict=True):
            wrap = jnp.where(z + offset < 0, -1, jnp.where(z + offset >= 16, 1, 0))
            held = slot + wrap
            valid = (held >= 0) & (held < 2)
            start = pl.multiple_of(jnp.clip(held, 0, 1) * 256, 256)
            starts.append(start)
            key = ref[0, pl.ds(start, 256), :]
            part = lax.dot_general(query, key, (((1,), (1,)), ((), ())), preferred_element_type=F32)
            scores.append(part + jnp.where(valid, 0.0, -jnp.inf))
        top = scores[0]
        for part in scores[1:]:
            top = jnp.maximum(top, part)
        top = jnp.max(top, axis=-1, keepdims=True)
        total = jnp.zeros((256, 1), F32)
        mixed = jnp.zeros((256, HD), F32)
        for part, start, ref in zip(scores, starts, kvs, strict=True):
            expd = jnp.exp(part - top)
            total += jnp.sum(expd, axis=-1, keepdims=True)
            value = ref[1, pl.ds(start, 256), :]
            mixed += jnp.dot(expd.astype(BF), value, preferred_element_type=F32)
        result = (mixed / total).astype(BF)
        for copy in range(4):
            out_ref[copy, slot * 256 : (slot + 1) * 256, :] = result


def attend(place, query, kvs):
    return pl.pallas_call(
        attend_kernel,
        out_shape=jax.ShapeDtypeStruct((4, 512, HD), BF),
        in_specs=[pl.BlockSpec(memory_space=pltpu.SMEM)] + [pl.BlockSpec(memory_space=pltpu.VMEM)] * 6,
        out_specs=pl.BlockSpec(memory_space=pltpu.VMEM),
        compiler_params=pltpu.CompilerParams(vmem_limit_bytes=32 << 20),
        cost_estimate=pl.CostEstimate(flops=4 * 512 * 1280 * HD, bytes_accessed=1_600_000, transcendentals=512 * 1280),
    )(place, query, *kvs)


def out_kernel(place_ref, heads_ref, others_ref, weights_ref, out_ref):
    first = place_ref[4] == 0
    corner = 12 + 8 * lax.rem(place_ref[2], 2)
    for slot in range(2):
        part = jnp.zeros((256, 768), F32)
        for x in range(4):
            rows = slice(slot * 256, (slot + 1) * 256)
            held, far = heads_ref[x, rows, :], others_ref[x, rows, :]
            pair = jnp.concatenate([jnp.where(first, held, far), jnp.where(first, far, held)], axis=1)
            block = jnp.concatenate([weights_ref[lax.rem(corner + 4 * r + x, 16)] for r in range(4)], axis=0)
            part += lax.dot_general(pair, block, (((1,), (1,)), ((), ())), preferred_element_type=F32)
        out_ref[slot] = part[:, :384].astype(BF)
        out_ref[2 + slot] = part[:, 384:].astype(BF)


def project_out(place, heads, others, weights):
    return pl.pallas_call(
        out_kernel,
        out_shape=jax.ShapeDtypeStruct((4, 256, 384), BF),
        in_specs=[pl.BlockSpec(memory_space=pltpu.SMEM)] + [pl.BlockSpec(memory_space=pltpu.VMEM)] * 3,
        out_specs=pl.BlockSpec(memory_space=pltpu.VMEM),
        compiler_params=pltpu.CompilerParams(vmem_limit_bytes=32 << 20),
        cost_estimate=pl.CostEstimate(flops=2 * 512 * 768 * 1024, bytes_accessed=3_500_000, transcendentals=0),
    )(place, heads, others, weights)


def per_device(patches, ln_gain, w_query, w_key, w_value, query_gain, key_gain, w_out):
    place = jnp.stack([lax.axis_index(a) for a in AXES]).astype(jnp.int32)
    ylo, core = place[0], place[4]
    home = core == ylo
    acts = lax.all_gather(patches, ("ylo", "x", "yh", "core"), axis=0, tiled=False)

    held = jnp.stack([w_query, w_key, w_value])
    got = send(held, cross)
    one = jnp.where(home, held, got)
    two = jnp.where(home, got, send(got, from_home))
    shards = [[], []]
    ends = [one, two]
    for step in range(7):
        for chain in range(2):
            ends[chain] = send(ends[chain], onward)
            shards[chain].append(ends[chain])
    last = send(jnp.where(core == 0, ends[0], ends[1]), onward)
    own = jnp.where(core == 0, one, two)

    turned = send(w_out.T, out_weight)
    out_weights = lax.all_gather(turned, "z", axis=0, tiled=False)

    normed = normalise(place, acts, ln_gain)
    gains = jnp.pad(jnp.stack([query_gain, key_gain]), ((0, 6), (0, 128)))
    mine, theirs = multiply(place, gains, normed, shards[0] + shards[1] + [own, last])
    query, kv = split_heads(place, mine, send(theirs, other_core), gains)
    near = {offset: send(kv, along_z(-offset)) for offset in (-2, 2, -1, 1)}
    near[0] = kv
    attended = attend(place, query, [near[o] for o in (-2, -1, 0, 1, 2)])
    heads = lax.all_to_all(attended, "x", 0, 0, tiled=True)
    parts = project_out(place, heads, send(heads, other_core), out_weights)
    parts = lax.all_to_all(parts, ("yh", "ylo"), 0, 0, tiled=True)
    return jnp.sum(parts.astype(F32), axis=0).astype(BF)


def solution(mesh):
    fine = Mesh(mesh.devices.reshape(SIZES), AXES)
    tm, tensor = ("ylo", "z"), ("x", "yh", "core")
    return jax.shard_map(
        per_device,
        mesh=fine,
        in_specs=(
            P(tm, tensor),
            P(),
            P(tm, tensor),
            P(tm, tensor),
            P(tm, tensor),
            P(tensor),
            P(tensor),
            P(tensor, tm),
        ),
        out_specs=P(tm, tensor),
        check_vma=False,
    )
```

```python
import functools

import jax
import jax.numpy as jnp
from jax import lax
from jax.experimental import pallas as pl
from jax.experimental.pallas import tpu as pltpu
from jax.sharding import Mesh
from jax.sharding import PartitionSpec as P

HD = 128
EPS = 1e-06
AXES = ("ylo", "z", "x", "yh", "core")
SIZES = (2, 16, 4, 2, 2)
ROWS = 192
WIDTH = 6144
WINDOW = 9 * 384
BF = jnp.bfloat16
F32 = jnp.float32


def _places():
    for ylo in range(2):
        for z in range(16):
            for x in range(4):
                for yh in range(2):
                    for core in range(2):
                        yield ylo, z, x, yh, core


def _number(ylo, z, x, yh, core):
    return (((ylo * 16 + z) * 4 + x) * 2 + yh) * 2 + core


def send(value, target):
    pairs = [(_number(*p), _number(*target(*p))) for p in _places() if target(*p) is not None]
    return lax.ppermute(value, AXES, pairs)


def along_z(by):
    return lambda ylo, z, x, yh, core: (ylo, (z + by) % 16, x, yh, core)


def other_core(ylo, z, x, yh, core):
    return ylo, z, x, yh, 1 - core


def cross(ylo, z, x, yh, core):
    return (ylo, z, x, yh, 1 - core) if core == ylo else (core, z, x, yh, core)


def from_home(ylo, z, x, yh, core):
    return (ylo, z, x, yh, 1 - core) if core == ylo else None


def onward(ylo, z, x, yh, core):
    return ylo, (z + 1 - 2 * core) % 16, x, yh, core


def out_weight(ylo, z, x, yh, core):
    low = z % 8
    nearby = z - low - 4 + 4 * (low % 2 + 2 * (low // 4)) + x
    return core, nearby % 16, ylo * 2 + z // 8, yh, (z // 2) % 2


def norm_kernel(place_ref, acts_ref, gain_ref, out_ref):
    ylo, z, core = place_ref[0], place_ref[1], place_ref[4]
    total = jnp.zeros((acts_ref.shape[2], 1), F32)
    for t in range(16):
        total += jnp.sum(acts_ref[0, t].astype(F32), axis=-1, keepdims=True)
    mean = total / WIDTH
    spread = jnp.zeros_like(total)
    for t in range(16):
        centred = acts_ref[0, t].astype(F32) - mean
        spread += jnp.sum(centred * centred, axis=-1, keepdims=True)
    scale = lax.rsqrt(spread / WIDTH + EPS)
    large = lax.rem(z + 8 * (1 - core), 16) // 2
    small = lax.rem(z + 1 + 8 * (1 - core), 16) // 2
    for i in range(9):
        if i < 5:
            t = (ylo ^ core) * 8 + lax.rem(large + i, 8)
        else:
            t = (ylo ^ (1 - core)) * 8 + lax.rem(small + i - 5, 8)
        centred = acts_ref[0, t].astype(F32) - mean
        gain = gain_ref[pl.ds(t, 1), :]
        out_ref[:, i * 384 : (i + 1) * 384] = (centred * scale * gain).astype(BF)


def normalise(place, acts, gain):
    rows = 64
    return pl.pallas_call(
        norm_kernel,
        grid=(2, 256 // rows),
        out_shape=jax.ShapeDtypeStruct((512, WINDOW), BF),
        in_specs=[
            pl.BlockSpec(memory_space=pltpu.SMEM),
            pl.BlockSpec((1, 16, rows, 384), lambda s, r: (s, 0, r, 0)),
            pl.BlockSpec((16, 384), lambda s, r: (0, 0)),
        ],
        out_specs=pl.BlockSpec((rows, WINDOW), lambda s, r: (s * (256 // rows) + r, 0)),
        compiler_params=pltpu.CompilerParams(vmem_limit_bytes=60 << 20),
        cost_estimate=pl.CostEstimate(flops=30_000_000, bytes_accessed=10_000_000, transcendentals=0),
    )(place, acts.reshape(2, 16, 256, 384), gain.reshape(16, 384))


def head_norm(raw, gain):
    mean = jnp.mean(raw, axis=-1, keepdims=True)
    centred = raw - mean
    spread = jnp.mean(centred * centred, axis=-1, keepdims=True)
    return centred * lax.rsqrt(spread + EPS) * gain


def product_kernel(place_ref, gains_ref, normed_ref, *refs):
    first, second, own, last = refs[:7], refs[7:14], refs[14], refs[15]
    mine_ref, theirs_ref, weights, sem = refs[16:]
    core = place_ref[4]

    @pl.when(pl.program_id(0) == 0)
    def _():
        odd = lax.rem(place_ref[1], 2)
        up = core == 0
        blocks = [(own, odd + jnp.where(up, 8, 0)), (last, odd + jnp.where(up, 0, 8))]
        for i in range(7):
            n = i + 1
            blocks.append((first[i], jnp.where(up, odd + 8 - n, 11 - odd + n - 1)))
            blocks.append((second[i], jnp.where(up, 11 - odd + 7 - n, odd + n)))
        copies = []
        for ref, block in blocks:
            rows = pl.ds(pl.multiple_of(block * ROWS, ROWS), ROWS)
            for m in range(3):
                copies.append(pltpu.make_async_copy(ref.at[m], weights.at[rows, pl.ds(m * 256, 256)], sem.at[len(copies)]))
        for copy in copies:
            copy.start()
        for block in (9 * (1 - odd), 10 + 7 * odd):
            weights[pl.ds(pl.multiple_of(block * ROWS, ROWS), ROWS), :] = jnp.zeros((ROWS, 768), BF)
        for copy in copies:
            copy.wait()

    raw = jnp.dot(normed_ref[...], weights[...], preferred_element_type=F32)
    for m in range(3):
        one, two = raw[:, m * 256 : m * 256 + HD], raw[:, m * 256 + HD : (m + 1) * 256]
        mine_ref[:, m * HD : (m + 1) * HD] = jnp.where(core == 0, one, two)
        theirs_ref[:128, m * HD : (m + 1) * HD] = jnp.where(core == 0, two, one)
    theirs_ref[128:, :] = gains_ref[...]


def multiply(place, gains, normed, shards):
    rows = 128
    return pl.pallas_call(
        product_kernel,
        grid=(512 // rows,),
        out_shape=[jax.ShapeDtypeStruct((512, 3 * HD), F32), jax.ShapeDtypeStruct((544, 3 * HD), F32)],
        in_specs=[pl.BlockSpec(memory_space=pltpu.SMEM), pl.BlockSpec((8, 3 * HD), lambda r: (0, 0)), pl.BlockSpec((rows, WINDOW), lambda r: (r, 0))]
        + [pl.BlockSpec(memory_space=pl.ANY)] * 16,
        out_specs=[pl.BlockSpec((n, 3 * HD), lambda r: (r, 0)) for n in (rows, rows + 8)],
        scratch_shapes=[pltpu.VMEM((WINDOW, 768), BF), pltpu.SemaphoreType.DMA((48,))],
        compiler_params=pltpu.CompilerParams(vmem_limit_bytes=32 << 20),
        cost_estimate=pl.CostEstimate(flops=2 * 512 * WINDOW * 768, bytes_accessed=10_000_000, transcendentals=0),
    )(place, gains, normed, *shards)


def heads_kernel(place_ref, mine_ref, theirs_ref, gains_ref, q_ref, kv_ref):
    ylo, core = place_ref[0], place_ref[4]
    pair = jnp.where(core == ylo, gains_ref[0:2, :256], theirs_ref[0, 128:130, :256])
    gains = jnp.where(core == 0, pair[:, :HD], pair[:, HD:])
    for r in range(4):
        rows = slice(r * 128, (r + 1) * 128)
        raw = mine_ref[rows, :] + theirs_ref[r, :128, :]
        query = head_norm(raw[:, :HD], gains[0:1, :]) * HD ** (-0.5)
        q_ref[rows, :] = query.astype(BF)
        kv_ref[0, rows, :] = head_norm(raw[:, HD : 2 * HD], gains[1:2, :]).astype(BF)
        kv_ref[1, rows, :] = raw[:, 2 * HD :].astype(BF)


def split_heads(place, mine, theirs, gains):
    return pl.pallas_call(
        heads_kernel,
        out_shape=(jax.ShapeDtypeStruct((512, HD), BF), jax.ShapeDtypeStruct((2, 512, HD), BF)),
        in_specs=[pl.BlockSpec(memory_space=pltpu.SMEM)] + [pl.BlockSpec(memory_space=pltpu.VMEM)] * 3,
        out_specs=(pl.BlockSpec(memory_space=pltpu.VMEM), pl.BlockSpec(memory_space=pltpu.VMEM)),
        compiler_params=pltpu.CompilerParams(vmem_limit_bytes=32 << 20),
        cost_estimate=pl.CostEstimate(flops=4_000_000, bytes_accessed=2_000_000, transcendentals=0),
    )(place, mine, theirs.reshape(4, 136, 3 * HD), gains)


def attend_kernel(place_ref, q_ref, *refs):
    kvs, out_ref = refs[:5], refs[5]
    z = place_ref[1]
    for slot in range(2):
        query = q_ref[slot * 256 : (slot + 1) * 256, :]
        scores = []
        starts = []
        for offset, ref in zip((-2, -1, 0, 1, 2), kvs, strict=True):
            wrap = jnp.where(z + offset < 0, -1, jnp.where(z + offset >= 16, 1, 0))
            held = slot + wrap
            valid = (held >= 0) & (held < 2)
            start = pl.multiple_of(jnp.clip(held, 0, 1) * 256, 256)
            starts.append(start)
            key = ref[0, pl.ds(start, 256), :]
            part = lax.dot_general(query, key, (((1,), (1,)), ((), ())), preferred_element_type=F32)
            scores.append(part + jnp.where(valid, 0.0, -jnp.inf))
        top = scores[0]
        for part in scores[1:]:
            top = jnp.maximum(top, part)
        top = jnp.max(top, axis=-1, keepdims=True)
        total = jnp.zeros((256, 1), F32)
        mixed = jnp.zeros((256, HD), F32)
        for part, start, ref in zip(scores, starts, kvs, strict=True):
            expd = jnp.exp(part - top)
            total += jnp.sum(expd, axis=-1, keepdims=True)
            value = ref[1, pl.ds(start, 256), :]
            mixed += jnp.dot(expd.astype(BF), value, preferred_element_type=F32)
        result = (mixed / total).astype(BF)
        for copy in range(4):
            out_ref[copy, slot * 256 : (slot + 1) * 256, :] = result


def attend(place, query, kvs):
    return pl.pallas_call(
        attend_kernel,
        out_shape=jax.ShapeDtypeStruct((4, 512, HD), BF),
        in_specs=[pl.BlockSpec(memory_space=pltpu.SMEM)] + [pl.BlockSpec(memory_space=pltpu.VMEM)] * 6,
        out_specs=pl.BlockSpec(memory_space=pltpu.VMEM),
        compiler_params=pltpu.CompilerParams(vmem_limit_bytes=32 << 20),
        cost_estimate=pl.CostEstimate(flops=4 * 512 * 1280 * HD, bytes_accessed=1_600_000, transcendentals=512 * 1280),
    )(place, query, *kvs)


def out_kernel(place_ref, heads_ref, others_ref, weights_ref, out_ref):
    first = place_ref[4] == 0
    corner = 12 + 8 * lax.rem(place_ref[2], 2)
    for slot in range(2):
        part = jnp.zeros((256, 768), F32)
        for x in range(4):
            rows = slice(slot * 256, (slot + 1) * 256)
            held, far = heads_ref[x, rows, :], others_ref[x, rows, :]
            pair = jnp.concatenate([jnp.where(first, held, far), jnp.where(first, far, held)], axis=1)
            block = jnp.concatenate([weights_ref[lax.rem(corner + 4 * r + x, 16)] for r in range(4)], axis=0)
            part += lax.dot_general(pair, block, (((1,), (1,)), ((), ())), preferred_element_type=F32)
        out_ref[slot] = part[:, :384].astype(BF)
        out_ref[2 + slot] = part[:, 384:].astype(BF)


def project_out(place, heads, others, weights):
    return pl.pallas_call(
        out_kernel,
        out_shape=jax.ShapeDtypeStruct((4, 256, 384), BF),
        in_specs=[pl.BlockSpec(memory_space=pltpu.SMEM)] + [pl.BlockSpec(memory_space=pltpu.VMEM)] * 3,
        out_specs=pl.BlockSpec(memory_space=pltpu.VMEM),
        compiler_params=pltpu.CompilerParams(vmem_limit_bytes=32 << 20),
        cost_estimate=pl.CostEstimate(flops=2 * 512 * 768 * 1024, bytes_accessed=3_500_000, transcendentals=0),
    )(place, heads, others, weights)


def per_device(patches, ln_gain, w_query, w_key, w_value, query_gain, key_gain, w_out):
    place = jnp.stack([lax.axis_index(a) for a in AXES]).astype(jnp.int32)
    ylo, core = place[0], place[4]
    home = core == ylo
    acts = lax.all_gather(patches, ("ylo", "x", "yh", "core"), axis=0, tiled=False)

    held = jnp.stack([w_query, w_key, w_value])
    got = send(held, cross)
    one = jnp.where(home, held, got)
    two = jnp.where(home, got, send(got, from_home))
    shards = [[], []]
    ends = [one, two]
    for step in range(7):
        for chain in range(2):
            ends[chain] = send(ends[chain], onward)
            shards[chain].append(ends[chain])
    last = send(jnp.where(core == 0, ends[0], ends[1]), onward)
    own = jnp.where(core == 0, one, two)

    turned = send(w_out.T, out_weight)
    out_weights = lax.all_gather(turned, "z", axis=0, tiled=False)

    normed = normalise(place, acts, ln_gain)
    gains = jnp.pad(jnp.stack([query_gain, key_gain]), ((0, 6), (0, 128)))
    mine, theirs = multiply(place, gains, normed, shards[0] + shards[1] + [own, last])
    query, kv = split_heads(place, mine, send(theirs, other_core), gains)
    near = {offset: send(kv, along_z(-offset)) for offset in (-2, 2, -1, 1)}
    near[0] = kv
    attended = attend(place, query, [near[o] for o in (-2, -1, 0, 1, 2)])
    heads = lax.all_to_all(attended, "x", 0, 0, tiled=True)
    parts = project_out(place, heads, send(heads, other_core), out_weights)
    parts = lax.all_to_all(parts, ("yh", "ylo"), 0, 0, tiled=True)
    return jnp.sum(parts.astype(F32), axis=0).astype(BF)


def solution(mesh):
    fine = Mesh(mesh.devices.reshape(SIZES), AXES)
    tm, tensor = ("ylo", "z"), ("x", "yh", "core")
    return jax.shard_map(
        per_device,
        mesh=fine,
        in_specs=(
            P(tm, tensor),
            P(),
            P(tm, tensor),
            P(tm, tensor),
            P(tm, tensor),
            P(tensor),
            P(tensor),
            P(tensor, tm),
        ),
        out_specs=P(tm, tensor),
        check_vma=False,
    )
```

```python
import functools

import jax
import jax.numpy as jnp
from jax import lax
from jax.experimental import pallas as pl
from jax.experimental.pallas import tpu as pltpu
from jax.sharding import Mesh
from jax.sharding import PartitionSpec as P

HD = 128
EPS = 1e-06
AXES = ("ylo", "z", "x", "yh", "core")
SIZES = (2, 16, 4, 2, 2)
ROWS = 192
WIDTH = 6144
WINDOW = 9 * 384
BF = jnp.bfloat16
F32 = jnp.float32


def _places():
    for ylo in range(2):
        for z in range(16):
            for x in range(4):
                for yh in range(2):
                    for core in range(2):
                        yield ylo, z, x, yh, core


def _number(ylo, z, x, yh, core):
    return (((ylo * 16 + z) * 4 + x) * 2 + yh) * 2 + core


def send(value, target):
    pairs = [(_number(*p), _number(*target(*p))) for p in _places() if target(*p) is not None]
    return lax.ppermute(value, AXES, pairs)


def along_z(by):
    return lambda ylo, z, x, yh, core: (ylo, (z + by) % 16, x, yh, core)


def other_core(ylo, z, x, yh, core):
    return ylo, z, x, yh, 1 - core


def cross(ylo, z, x, yh, core):
    return (ylo, z, x, yh, 1 - core) if core == ylo else (core, z, x, yh, core)


def from_home(ylo, z, x, yh, core):
    return (ylo, z, x, yh, 1 - core) if core == ylo else None


def onward(ylo, z, x, yh, core):
    return ylo, (z + 1 - 2 * core) % 16, x, yh, core


def out_weight(ylo, z, x, yh, core):
    low = z % 8
    nearby = z - low - 4 + 4 * (low % 2 + 2 * (low // 4)) + x
    return core, nearby % 16, ylo * 2 + z // 8, yh, (z // 2) % 2


def norm_kernel(place_ref, acts_ref, gain_ref, out_ref):
    ylo, z, core = place_ref[0], place_ref[1], place_ref[4]
    total = jnp.zeros((acts_ref.shape[2], 1), F32)
    for t in range(16):
        total += jnp.sum(acts_ref[0, t].astype(F32), axis=-1, keepdims=True)
    mean = total / WIDTH
    spread = jnp.zeros_like(total)
    for t in range(16):
        centred = acts_ref[0, t].astype(F32) - mean
        spread += jnp.sum(centred * centred, axis=-1, keepdims=True)
    scale = lax.rsqrt(spread / WIDTH + EPS)
    large = lax.rem(z + 8 * (1 - core), 16) // 2
    small = lax.rem(z + 1 + 8 * (1 - core), 16) // 2
    for i in range(9):
        if i < 5:
            t = (ylo ^ core) * 8 + lax.rem(large + i, 8)
        else:
            t = (ylo ^ (1 - core)) * 8 + lax.rem(small + i - 5, 8)
        centred = acts_ref[0, t].astype(F32) - mean
        gain = gain_ref[pl.ds(t, 1), :]
        out_ref[:, i * 384 : (i + 1) * 384] = (centred * scale * gain).astype(BF)


def normalise(place, acts, gain):
    rows = 64
    return pl.pallas_call(
        norm_kernel,
        grid=(2, 256 // rows),
        out_shape=jax.ShapeDtypeStruct((512, WINDOW), BF),
        in_specs=[
            pl.BlockSpec(memory_space=pltpu.SMEM),
            pl.BlockSpec((1, 16, rows, 384), lambda s, r: (s, 0, r, 0)),
            pl.BlockSpec((16, 384), lambda s, r: (0, 0)),
        ],
        out_specs=pl.BlockSpec((rows, WINDOW), lambda s, r: (s * (256 // rows) + r, 0)),
        compiler_params=pltpu.CompilerParams(vmem_limit_bytes=16 << 20),
        cost_estimate=pl.CostEstimate(flops=30_000_000, bytes_accessed=10_000_000, transcendentals=0),
    )(place, acts.reshape(2, 16, 256, 384), gain.reshape(16, 384))


def head_norm(raw, gain):
    mean = jnp.mean(raw, axis=-1, keepdims=True)
    centred = raw - mean
    spread = jnp.mean(centred * centred, axis=-1, keepdims=True)
    return centred * lax.rsqrt(spread + EPS) * gain


def product_kernel(place_ref, gains_ref, normed_ref, *refs):
    first, second, own, last = refs[:7], refs[7:14], refs[14], refs[15]
    mine_ref, theirs_ref, weights, sem = refs[16:]
    core = place_ref[4]

    @pl.when(pl.program_id(0) == 0)
    def _():
        odd = lax.rem(place_ref[1], 2)
        up = core == 0
        blocks = [(own, odd + jnp.where(up, 8, 0)), (last, odd + jnp.where(up, 0, 8))]
        for i in range(7):
            n = i + 1
            blocks.append((first[i], jnp.where(up, odd + 8 - n, 11 - odd + n - 1)))
            blocks.append((second[i], jnp.where(up, 11 - odd + 7 - n, odd + n)))
        copies = []
        for ref, block in blocks:
            rows = pl.ds(pl.multiple_of(block * ROWS, ROWS), ROWS)
            for m in range(3):
                copies.append(pltpu.make_async_copy(ref.at[m], weights.at[rows, pl.ds(m * 256, 256)], sem.at[len(copies)]))
        for copy in copies:
            copy.start()
        for block in (9 * (1 - odd), 10 + 7 * odd):
            weights[pl.ds(pl.multiple_of(block * ROWS, ROWS), ROWS), :] = jnp.zeros((ROWS, 768), BF)
        for copy in copies:
            copy.wait()

    raw = jnp.dot(normed_ref[...], weights[...], preferred_element_type=F32)
    for m in range(3):
        one, two = raw[:, m * 256 : m * 256 + HD], raw[:, m * 256 + HD : (m + 1) * 256]
        mine_ref[:, m * HD : (m + 1) * HD] = jnp.where(core == 0, one, two)
        theirs_ref[:128, m * HD : (m + 1) * HD] = jnp.where(core == 0, two, one)
    theirs_ref[128:, :] = gains_ref[...]


def multiply(place, gains, normed, shards):
    rows = 128
    return pl.pallas_call(
        product_kernel,
        grid=(512 // rows,),
        out_shape=[jax.ShapeDtypeStruct((512, 3 * HD), F32), jax.ShapeDtypeStruct((544, 3 * HD), F32)],
        in_specs=[pl.BlockSpec(memory_space=pltpu.SMEM), pl.BlockSpec((8, 3 * HD), lambda r: (0, 0)), pl.BlockSpec((rows, WINDOW), lambda r: (r, 0))]
        + [pl.BlockSpec(memory_space=pl.ANY)] * 16,
        out_specs=[pl.BlockSpec((n, 3 * HD), lambda r: (r, 0)) for n in (rows, rows + 8)],
        scratch_shapes=[pltpu.VMEM((WINDOW, 768), BF), pltpu.SemaphoreType.DMA((48,))],
        compiler_params=pltpu.CompilerParams(vmem_limit_bytes=16 << 20),
        cost_estimate=pl.CostEstimate(flops=2 * 512 * WINDOW * 768, bytes_accessed=10_000_000, transcendentals=0),
    )(place, gains, normed, *shards)


def heads_kernel(place_ref, mine_ref, theirs_ref, gains_ref, q_ref, kv_ref):
    ylo, core = place_ref[0], place_ref[4]
    pair = jnp.where(core == ylo, gains_ref[0:2, :256], theirs_ref[0, 128:130, :256])
    gains = jnp.where(core == 0, pair[:, :HD], pair[:, HD:])
    for r in range(4):
        rows = slice(r * 128, (r + 1) * 128)
        raw = mine_ref[rows, :] + theirs_ref[r, :128, :]
        query = head_norm(raw[:, :HD], gains[0:1, :]) * HD ** (-0.5)
        q_ref[rows, :] = query.astype(BF)
        kv_ref[0, rows, :] = head_norm(raw[:, HD : 2 * HD], gains[1:2, :]).astype(BF)
        kv_ref[1, rows, :] = raw[:, 2 * HD :].astype(BF)


def split_heads(place, mine, theirs, gains):
    return pl.pallas_call(
        heads_kernel,
        out_shape=(jax.ShapeDtypeStruct((512, HD), BF), jax.ShapeDtypeStruct((2, 512, HD), BF)),
        in_specs=[pl.BlockSpec(memory_space=pltpu.SMEM)] + [pl.BlockSpec(memory_space=pltpu.VMEM)] * 3,
        out_specs=(pl.BlockSpec(memory_space=pltpu.VMEM), pl.BlockSpec(memory_space=pltpu.VMEM)),
        compiler_params=pltpu.CompilerParams(vmem_limit_bytes=16 << 20),
        cost_estimate=pl.CostEstimate(flops=4_000_000, bytes_accessed=2_000_000, transcendentals=0),
    )(place, mine, theirs.reshape(4, 136, 3 * HD), gains)


def attend_kernel(place_ref, q_ref, *refs):
    kvs, out_ref = refs[:5], refs[5]
    z = place_ref[1]
    for slot in range(2):
        query = q_ref[slot * 256 : (slot + 1) * 256, :]
        scores = []
        starts = []
        for offset, ref in zip((-2, -1, 0, 1, 2), kvs, strict=True):
            wrap = jnp.where(z + offset < 0, -1, jnp.where(z + offset >= 16, 1, 0))
            held = slot + wrap
            valid = (held >= 0) & (held < 2)
            start = pl.multiple_of(jnp.clip(held, 0, 1) * 256, 256)
            starts.append(start)
            key = ref[0, pl.ds(start, 256), :]
            part = lax.dot_general(query, key, (((1,), (1,)), ((), ())), preferred_element_type=F32)
            scores.append(part + jnp.where(valid, 0.0, -jnp.inf))
        top = scores[0]
        for part in scores[1:]:
            top = jnp.maximum(top, part)
        top = jnp.max(top, axis=-1, keepdims=True)
        total = jnp.zeros((256, 1), F32)
        mixed = jnp.zeros((256, HD), F32)
        for part, start, ref in zip(scores, starts, kvs, strict=True):
            expd = jnp.exp(part - top)
            total += jnp.sum(expd, axis=-1, keepdims=True)
            value = ref[1, pl.ds(start, 256), :]
            mixed += jnp.dot(expd.astype(BF), value, preferred_element_type=F32)
        result = (mixed / total).astype(BF)
        for copy in range(4):
            out_ref[copy, slot * 256 : (slot + 1) * 256, :] = result


def attend(place, query, kvs):
    return pl.pallas_call(
        attend_kernel,
        out_shape=jax.ShapeDtypeStruct((4, 512, HD), BF),
        in_specs=[pl.BlockSpec(memory_space=pltpu.SMEM)] + [pl.BlockSpec(memory_space=pltpu.VMEM)] * 6,
        out_specs=pl.BlockSpec(memory_space=pltpu.VMEM),
        compiler_params=pltpu.CompilerParams(vmem_limit_bytes=16 << 20),
        cost_estimate=pl.CostEstimate(flops=4 * 512 * 1280 * HD, bytes_accessed=1_600_000, transcendentals=512 * 1280),
    )(place, query, *kvs)


def out_kernel(place_ref, heads_ref, others_ref, weights_ref, out_ref):
    first = place_ref[4] == 0
    corner = 12 + 8 * lax.rem(place_ref[2], 2)
    for slot in range(2):
        part = jnp.zeros((256, 768), F32)
        for x in range(4):
            rows = slice(slot * 256, (slot + 1) * 256)
            held, far = heads_ref[x, rows, :], others_ref[x, rows, :]
            pair = jnp.concatenate([jnp.where(first, held, far), jnp.where(first, far, held)], axis=1)
            block = jnp.concatenate([weights_ref[lax.rem(corner + 4 * r + x, 16)] for r in range(4)], axis=0)
            part += lax.dot_general(pair, block, (((1,), (1,)), ((), ())), preferred_element_type=F32)
        out_ref[slot] = part[:, :384].astype(BF)
        out_ref[2 + slot] = part[:, 384:].astype(BF)


def project_out(place, heads, others, weights):
    return pl.pallas_call(
        out_kernel,
        out_shape=jax.ShapeDtypeStruct((4, 256, 384), BF),
        in_specs=[pl.BlockSpec(memory_space=pltpu.SMEM)] + [pl.BlockSpec(memory_space=pltpu.VMEM)] * 3,
        out_specs=pl.BlockSpec(memory_space=pltpu.VMEM),
        compiler_params=pltpu.CompilerParams(vmem_limit_bytes=16 << 20),
        cost_estimate=pl.CostEstimate(flops=2 * 512 * 768 * 1024, bytes_accessed=3_500_000, transcendentals=0),
    )(place, heads, others, weights)


def per_device(patches, ln_gain, w_query, w_key, w_value, query_gain, key_gain, w_out):
    place = jnp.stack([lax.axis_index(a) for a in AXES]).astype(jnp.int32)
    ylo, core = place[0], place[4]
    home = core == ylo
    acts = lax.all_gather(patches, ("ylo", "x", "yh", "core"), axis=0, tiled=False)

    held = jnp.stack([w_query, w_key, w_value])
    got = send(held, cross)
    one = jnp.where(home, held, got)
    two = jnp.where(home, got, send(got, from_home))
    shards = [[], []]
    ends = [one, two]
    for step in range(7):
        for chain in range(2):
            ends[chain] = send(ends[chain], onward)
            shards[chain].append(ends[chain])
    last = send(jnp.where(core == 0, ends[0], ends[1]), onward)
    own = jnp.where(core == 0, one, two)

    turned = send(w_out.T, out_weight)
    out_weights = lax.all_gather(turned, "z", axis=0, tiled=False)

    normed = normalise(place, acts, ln_gain)
    gains = jnp.pad(jnp.stack([query_gain, key_gain]), ((0, 6), (0, 128)))
    mine, theirs = multiply(place, gains, normed, shards[0] + shards[1] + [own, last])
    query, kv = split_heads(place, mine, send(theirs, other_core), gains)
    near = {offset: send(kv, along_z(-offset)) for offset in (-2, 2, -1, 1)}
    near[0] = kv
    attended = attend(place, query, [near[o] for o in (-2, -1, 0, 1, 2)])
    heads = lax.all_to_all(attended, "x", 0, 0, tiled=True)
    parts = project_out(place, heads, send(heads, other_core), out_weights)
    parts = lax.all_to_all(parts, ("yh", "ylo"), 0, 0, tiled=True)
    return jnp.sum(parts.astype(F32), axis=0).astype(BF)


def solution(mesh):
    fine = Mesh(mesh.devices.reshape(SIZES), AXES)
    tm, tensor = ("ylo", "z"), ("x", "yh", "core")
    return jax.shard_map(
        per_device,
        mesh=fine,
        in_specs=(
            P(tm, tensor),
            P(),
            P(tm, tensor),
            P(tm, tensor),
            P(tm, tensor),
            P(tensor),
            P(tensor),
            P(tensor, tm),
        ),
        out_specs=P(tm, tensor),
        check_vma=False,
    )
```
